32 devices in a mesh: groups: 2 (over y), dom: 4 (over z), slab: 2 (over x), sub: 2 (over core).
Axes of the slice: x: 2, y: 2, z: 4, core: 2. Of those that a mesh axis runs over, the one named last changes fastest.
Arguments:
- volume: float32 [2, 65536, 512], P(None, ('groups', 'dom', 'slab')), parts along dimension 1, may hold values from -6 to 6
- interp: bfloat16 [8, 2, 4, 512, 128], P('dom', 'slab'), may hold values from -0.09375 to 0.09375
- fetch_lists: int32 [8, 2, 4, 12], P(('groups', 'dom'), 'slab'), parts along dimension 0, may hold values from 0 to 4095, as said below
- slot_of: int32 [16, 2, 512, 4], P(('groups', 'dom'), 'slab', 'sub'), parts along dimension 0, may hold values from 0 to 47
- images: bfloat16 [1, 32, 512, 2, 128], P(None, ('groups', 'dom'), 'sub'), parts along dimension 1, may hold values from -6 to 6
- particle_bin: int32 [1, 32], P(None, ('groups', 'dom')), parts along dimension 1, may hold values from 0 to 7, as said below
- ctf_class: int32 [1, 32], P(None, ('groups', 'dom')), parts along dimension 1, may hold values from 0 to 7
- defocus: float32 [8], replicated, may hold values from 20 to 200
Outputs:
- new_volume: float32 [2, 65536, 512], P(None, ('groups', 'dom', 'slab')), parts along dimension 1
The draws below stay inside these ranges and needn't reach their ends.
There are 2 independent parts, one for each index of `groups`. The reference program is written for one: setup_inputs(seed, part) draws one part's arguments, and reference() takes and returns one part's arrays. A program takes and returns all parts, laid end to end along the dimension named above; an argument that names none is the same for every part. Nothing has to cross between parts.
Inputs may be any that keep to these rules, and one draw needn't show every extreme that they name: fetch_lists[i, s, o, :] holds 12 distinct local indices of the tiles that dom index o holds in slab s. `particle_bin`: the particles of dom index i lie in bins i * 2 to (i + 1) * 2 - 1.
All inputs are finite; a program needn't handle non-finite values.
Results may differ from the reference program's by a relative error of at most 0.00044.
Values may be sent and summed in bfloat16 or wider, within the bound.
A program may use at most 128 MiB of HBM per device.

```python
import math
import jax
import jax.numpy as jnp
import numpy as np
from jax import lax

L = 256
TV = 512
PT = 128
K = 4
C = 12
NCTF = 8
STEPS = 1
BINS_DEV = 2
P_DEV = 4
N_TILES = 32768
TILES_DEV = 4096
JT = 512
BINS = 8
PARTICLES = 16
N_DOM = 4
N_SLAB = 2


def draw_fetch_lists(key, part):
    key = jax.random.fold_in(key, 11)
    limit = max(2, 2 ** 30 // TILES_DEV)
    scores = jax.random.randint(key, (N_DOM, N_SLAB, N_DOM, TILES_DEV), 0, limit) * TILES_DEV
    scores = scores + jnp.arange(TILES_DEV, dtype=jnp.int32)
    order = jnp.argsort(scores, axis=-1)
    return order[..., :C].astype(jnp.int32)


def draw_particle_bin(key, part):
    key = jax.random.fold_in(key, 12)
    offsets = jax.random.randint(key, (STEPS, PARTICLES), 0, BINS_DEV)
    position = jnp.arange(PARTICLES, dtype=jnp.int32)
    offsets = jnp.where(position % P_DEV == 0, BINS_DEV - 1, offsets)
    offsets = jnp.where(position % P_DEV == 1, 0, offsets)
    owner = position // P_DEV
    return (owner[None, :] * BINS_DEV + offsets).astype(jnp.int32)


def with_ends(values, own_key, least, largest):
    shape = values.shape
    index_at = [jax.random.randint(jax.random.fold_in(own_key, axis), (), 0, shape[axis]) for axis in range(len(shape))]
    values = values.at[tuple(index_at)].set(least)
    longest = shape.index(max(shape))
    index_at[longest] = (index_at[longest] + 1) % shape[longest]
    return values.at[tuple(index_at)].set(largest)


def block_scale(own_key, shape, pieces, smallest, high):
    gain = 1.0
    for dim, parts in pieces:
        draws = jax.random.uniform(jax.random.fold_in(jax.random.fold_in(own_key, 6), dim), (parts,), jnp.float32, smallest / len(pieces), high / len(pieces))
        gain = gain * jnp.repeat(jnp.exp(draws), shape[dim] // parts).reshape((-1,) + (1,) * (len(shape) - 1 - dim))
    return gain


def rank_table(number_of, lean):
    portions = [(1 << 20) // math.isqrt(standing ** lean) + 1 for standing in range(1, number_of + 1)]
    deviation = 1 + sum(portions) // (1 << 30)
    return np.cumsum(np.array([max(1, weight // deviation) for weight in portions]))


def ranked_ids(rng, dims, count, slope):
    grid = rank_table(count, slope)
    ticket = jax.random.randint(jax.random.fold_in(rng, 1), dims, 0, int(grid[count - 1]))
    grade = jnp.searchsorted(jnp.asarray(grid, jnp.int32), ticket, side="right")
    return jax.random.permutation(jax.random.fold_in(rng, 2), count)[grade].astype(jnp.int32)


def gaussian(own_key, dims, scale, reach, shards=(), held_as=jnp.bfloat16):
    loudness = block_scale(own_key, dims, shards, -0.22, 0.18) if shards else 1.0
    values = jax.random.normal(own_key, dims, jnp.float32) * scale * loudness
    return jnp.minimum(jnp.maximum(values, -reach), reach).astype(held_as)


def setup_inputs(seed: int = 0, part: int = 0) -> dict:
    seeds = jax.random.split(jax.random.key(seed), 9)
    part_keys = jax.random.split(jax.random.fold_in(seeds[8], part), 9)
    return {
        "volume": gaussian(part_keys[0], (2, N_TILES, TV), 1.0, 6.0, ((1, 8),), jnp.float32),
        "interp": gaussian(seeds[1], (BINS, N_SLAB, K, TV, PT), (N_SLAB * K * TV) ** -0.5, 0.09375, ((0, 4), (1, 2))),
        "fetch_lists": draw_fetch_lists(jax.random.fold_in(jax.random.fold_in(seeds[8], part), 71), part),
        "slot_of": with_ends(ranked_ids(part_keys[3], (BINS, N_SLAB, JT, K), N_DOM * C, 1), jax.random.fold_in(part_keys[3], 3), 0, (N_DOM * C) - 1).astype(jnp.int32),
        "images": gaussian(part_keys[4], (STEPS, PARTICLES, JT, 2, PT), 1.0, 6.0, ((1, 4), (2, 2))),
        "particle_bin": draw_particle_bin(jax.random.fold_in(jax.random.fold_in(seeds[8], part), 71), part),
        "ctf_class": with_ends(jax.random.randint(part_keys[6], (STEPS, PARTICLES), 0, NCTF), jax.random.fold_in(part_keys[6], 1), 0, NCTF - 1).astype(jnp.int32),
        "defocus": jnp.clip(jnp.exp(jax.random.uniform(seeds[7], (NCTF,), jnp.float32, math.log(20.0), math.log(200.0))), 20.0, 200.0),
    }


step_rate = 0.3
phase_shift = 0.1


def radius_table(first_tile, tile_count, pixel_width):
    tile_index = first_tile + jnp.arange(tile_count, dtype=jnp.int32)
    pixels = jnp.arange(pixel_width, dtype=jnp.int32)
    row_index = (tile_index * pixel_width) // L
    col_start = (tile_index * pixel_width) % L
    rowpos = (row_index - L // 2).astype(jnp.float32)[:, None]
    colpos = (col_start[:, None] + pixels[None, :] - L // 2).astype(jnp.float32)
    return (rowpos * rowpos + colpos * colpos) / float((L // 2) ** 2)


def reference(volume, interp, fetch_lists, slot_of, images, particle_bin, ctf_class, defocus):
    owner = slot_of // C
    within = slot_of % C
    requester = (jnp.arange(BINS, dtype=jnp.int32) // BINS_DEV)[:, None, None, None]
    slab_ids = jnp.arange(N_SLAB, dtype=jnp.int32)[None, :, None, None]
    local_ids = fetch_lists[requester, slab_ids, owner, within]
    tile_ids = ((owner * N_SLAB + slab_ids) * TILES_DEV + local_ids).astype(jnp.int32)
    radius = radius_table(0, JT, PT)
    current = volume
    for step_index in range(STEPS):
        packed = current.astype(jnp.bfloat16)

        def extract(bin_args):
            tiles_bin, weights_bin = bin_args
            gathered = jnp.take(packed, tiles_bin, axis=1).astype(jnp.float32)
            return jnp.einsum("xsjkv,skvq->jxq", gathered, weights_bin.astype(jnp.float32))

        slices = lax.map(extract, (tile_ids, interp))
        focus_value = defocus[ctf_class[step_index]]
        transfer = -jnp.sin(focus_value[:, None, None] * radius[None] + phase_shift)[:, :, None, :]
        picked = slices[particle_bin[step_index]]
        residual = transfer * picked - images[step_index].astype(jnp.float32)
        summed = jax.ops.segment_sum(transfer * residual, particle_bin[step_index], num_segments=BINS).astype(jnp.bfloat16)

        def scatter_bin(total, bin_args):
            tiles_bin, weights_bin, summed_bin = bin_args
            spread = jnp.einsum("jxq,skvq->xsjkv", summed_bin.astype(jnp.float32), weights_bin.astype(jnp.float32))
            return total.at[:, tiles_bin.reshape(-1)].add(spread.reshape(2, -1, TV)), None

        gradient, unused = lax.scan(scatter_bin, jnp.zeros_like(current), (tile_ids, interp, summed))
        current = current - step_rate * gradient
    return current
```

```python
import jax
import jax.numpy as jnp
from jax import lax
from jax.sharding import PartitionSpec as P

L = 256


step_rate = 0.3
phase_shift = 0.1


def radius_table(first_tile, tile_count, pixel_width):
    tile_index = first_tile + jnp.arange(tile_count, dtype=jnp.int32)
    pixels = jnp.arange(pixel_width, dtype=jnp.int32)
    row_index = tile_index * pixel_width // L
    col_start = tile_index * pixel_width % L
    rowpos = (row_index - L // 2).astype(jnp.float32)[:, None]
    colpos = (col_start[:, None] + pixels[None, :] - L // 2).astype(jnp.float32)
    return (rowpos * rowpos + colpos * colpos) / float((L // 2) ** 2)


def weigh_residual(slices, pictures, bin_local, classes, defocus, first_tile):
    tile_count = pictures.shape[1]
    pixel_width = pictures.shape[3]
    bin_count = slices.shape[0]
    radius = radius_table(first_tile, tile_count, pixel_width)
    class_match = classes[:, None] == jnp.arange(defocus.shape[0], dtype=jnp.int32)[None, :]
    focus_value = jnp.sum(jnp.where(class_match, defocus[None, :], 0.0), axis=1)
    transfer = -jnp.sin(focus_value[:, None, None] * radius[None] + phase_shift)[:, :, None, :]
    total = [0.0] * bin_count
    for p in range(pictures.shape[0]):
        picked = slices[0]
        for b in range(1, bin_count):
            picked = jnp.where(bin_local[p] == b, slices[b], picked)
        weighted = transfer[p] * (transfer[p] * picked - pictures[p].astype(jnp.float32))
        for b in range(bin_count):
            total[b] = total[b] + jnp.where(bin_local[p] == b, weighted, 0.0)
    return jnp.stack(total).astype(jnp.bfloat16)


def halves(x, n):
    parts = []
    for _ in range(n):
        part = x.astype(jnp.bfloat16)
        x = x - part.astype(jnp.float32)
        parts.append(part)
    return parts


def shards(volume, interp, fetch_lists, slot_of, images, particle_bin, ctf_class, defocus):
    dom_count = lax.axis_size("dom")
    wanted = fetch_lists[0, 0]
    capacity = wanted.shape[1]
    weights = interp[:, 0]
    bin_count = weights.shape[0]
    tile_width = weights.shape[2]
    slots = slot_of[:, 0]
    tile_count = slots.shape[1]
    listed = dom_count * capacity
    first_tile = lax.axis_index("sub") * tile_count
    asked_ids = lax.all_to_all(wanted, "dom", split_axis=0, concat_axis=0, tiled=True)
    asked_flat = asked_ids.reshape(-1)
    outgoing = jnp.take(volume, asked_flat, axis=1).astype(jnp.bfloat16)
    outgoing = outgoing.reshape(2, dom_count, capacity, tile_width)
    fetched = lax.all_to_all(outgoing, "dom", split_axis=1, concat_axis=1, tiled=True)
    fetched = fetched.reshape(2, listed, tile_width)
    table = jnp.einsum("xmv,bkvq->bkmxq", fetched, weights, preferred_element_type=jnp.float32)
    onehot = (slots[..., None] == jnp.arange(listed, dtype=jnp.int32)).astype(jnp.bfloat16)
    partial_value = sum(
        jnp.einsum("bjkm,bkmxq->bjxq", onehot, part, preferred_element_type=jnp.float32)
        for part in halves(table, 3)
    )
    pictures = images[0]
    bin_local = particle_bin[0] % bin_count
    slices = lax.psum(partial_value, "slab")
    summed = weigh_residual(slices, pictures, bin_local, ctf_class[0], defocus, first_tile)
    slot_sum = jnp.einsum("bjkm,bjxq->bkmxq", onehot, summed, preferred_element_type=jnp.float32)
    slot_grads = sum(
        jnp.einsum("bkmxq,bkvq->xmv", part, weights, preferred_element_type=jnp.float32)
        for part in halves(slot_sum, 3)
    )
    slot_grads = slot_grads.reshape(2, dom_count, capacity, tile_width)
    own_rows = lax.all_to_all(slot_grads, "dom", split_axis=1, concat_axis=1, tiled=True)
    row_grads = lax.psum(own_rows, "sub")
    return volume.at[:, asked_flat].add(-step_rate * row_grads.reshape(2, -1, tile_width))


def solution(mesh):
    in_specs = (
        P(None, ("groups", "dom", "slab"), None),
        P("dom", "slab", None, None, None),
        P(("groups", "dom"), "slab", None, None),
        P(("groups", "dom"), "slab", "sub", None),
        P(None, ("groups", "dom"), "sub", None, None),
        P(None, ("groups", "dom")),
        P(None, ("groups", "dom")),
        P(),
    )
    out_specs = P(None, ("groups", "dom", "slab"), None)
    return jax.shard_map(shards, mesh=mesh, in_specs=in_specs, out_specs=out_specs, check_vma=False)
```
